512 devices in a mesh: rep: 16 (over z_lo, x), seq: 8 (over y), tp: 4 (over z_hi, core).
Axes of the slice: x: 4, y: 8, z: 8 (z_hi: 2, z_lo: 4; z = z_hi * 4 + z_lo), core: 2. Of those that a mesh axis runs over, the one named last changes fastest.
Arguments:
- prompt_q: bfloat16 [2, 8192, 4096], P(None, ('rep', 'seq'), 'tp'), may hold values from -130 to 130
- prompt_k: bfloat16 [2, 8192, 512], P(None, ('rep', 'seq'), 'tp'), may hold values from -10 to 10
- prompt_v: bfloat16 [2, 8192, 512], P(None, ('rep', 'seq'), 'tp'), may hold values from -24 to 24
- dec_q: bfloat16 [640, 4, 4096], P('rep', None, 'tp'), may hold values from -130 to 130
- dec_k: bfloat16 [640, 4, 512], P('rep', None, 'tp'), may hold values from -9 to 9
- dec_v: bfloat16 [640, 4, 512], P('rep', None, 'tp'), may hold values from -24 to 24
Outputs:
- prefill_out: bfloat16 [2, 8192, 4096], P(None, ('rep', 'seq'), 'tp')
- decode_out: bfloat16 [640, 4, 4096], P('rep', None, 'tp')
The draws below stay inside these ranges and needn't reach their ends.
All inputs are finite; a program needn't handle non-finite values.
Results may differ from the reference program's by a relative error of at most 0.008.
Values may be sent and summed in bfloat16 or wider, within the bound.
A program may use at most 64 MiB of HBM per device.

```python
import math
import jax
import jax.numpy as jnp
from jax import lax

HEAD_WIDTH = 128
Q_HEADS = 32
KV_HEADS = 4
SAMPLES_PER_REP = 40
STEPS = 4
PROMPT = 16384
SAMPLES = 640


def shared_keys(key):
    half_rows = PROMPT // 2
    key_cols = KV_HEADS * HEAD_WIDTH
    normal_base = jnp.clip(jax.random.normal(key, (2, half_rows, key_cols), jnp.float32) * 1.5, -9.0, 9.0)
    pick_count = min(8, half_rows // 2 - 1)
    pick_rows = 2 * (jax.random.permutation(jax.random.fold_in(key, 101), half_rows // 2 - 1)[:pick_count] + 1)
    before = normal_base[0, pick_rows - 1]
    keys_out = normal_base.at[0, pick_rows - 1].set(before)
    return (keys_out, pick_rows)


def draw_prompt_k(key, part):
    keys_out, pick_rows = shared_keys(key)
    return keys_out.astype(jnp.bfloat16)


def draw_prompt_q(key, part):
    keys_out, pick_rows = shared_keys(key)
    key = jax.random.fold_in(key, 7)
    half_rows = PROMPT // 2
    normal_base = jnp.clip(jax.random.normal(key, (2, half_rows, Q_HEADS * HEAD_WIDTH), jnp.float32) * 1.5, -9.0, 9.0)
    current = normal_base[0, pick_rows]
    return normal_base.at[0, pick_rows].set(current).astype(jnp.bfloat16)


def draw_dec_q(key, part):
    key = jax.random.fold_in(key, 13)
    total_rows = SAMPLES * STEPS
    normal_base = jnp.clip(jax.random.normal(key, (total_rows, Q_HEADS * HEAD_WIDTH), jnp.float32) * 1.5, -9.0, 9.0)
    pick_count = min(8, total_rows)
    slot_list = jax.random.permutation(jax.random.fold_in(key, 17), total_rows)[:pick_count]
    current = normal_base[slot_list]
    normal_base = normal_base.at[slot_list].set(current)
    return normal_base.reshape(SAMPLES, STEPS, Q_HEADS * HEAD_WIDTH).astype(jnp.bfloat16)


def block_scale(key, shape, pieces, low, largest):
    def one(axis_at, parts):
        steps = jax.random.uniform(jax.random.fold_in(jax.random.fold_in(key, 6), axis_at), (parts,), jnp.float32, low / len(pieces), largest / len(pieces))
        return jnp.repeat(jnp.exp(steps), shape[axis_at] // parts).reshape((-1,) + (1,) * (len(shape) - axis_at - 1))

    gain = one(*pieces[0])
    for cut in pieces[1:]:
        gain = gain * one(*cut)
    return gain


def gaussian(key, dims, spread, limit, split=(), dtype=jnp.bfloat16):
    array = jax.random.normal(key, dims, jnp.float32) * spread
    if len(split) > 0:
        array = block_scale(key, dims, split, -0.22, 0.18) * array
    return jnp.clip(array, min=-limit, max=limit).astype(dtype)


def setup_inputs(seed: int = 0) -> dict:
    key_list = jax.random.split(jax.random.key(seed), 7)
    return {
        "prompt_q": draw_prompt_q(jax.random.fold_in(key_list[6], 71), 0),
        "prompt_k": draw_prompt_k(jax.random.fold_in(key_list[6], 71), 0),
        "prompt_v": gaussian(key_list[2], (2, PROMPT // 2, KV_HEADS * HEAD_WIDTH), 4.0, 24.0, ((1, 128), (2, 4))),
        "dec_q": draw_dec_q(jax.random.fold_in(key_list[6], 71), 0),
        "dec_k": gaussian(key_list[4], (SAMPLES, STEPS, KV_HEADS * HEAD_WIDTH), 1.5, 9.0, ((0, 16), (2, 4))),
        "dec_v": gaussian(key_list[5], (SAMPLES, STEPS, KV_HEADS * HEAD_WIDTH), 4.0, 24.0, ((0, 16), (2, 4))),
    }


def unfold(arr):
    return jnp.concatenate([arr[0], arr[1][::-1]], axis=0)

def refold(arr):
    half_rows = arr.shape[0] // 2
    return jnp.stack([arr[:half_rows], arr[half_rows:][::-1]], axis=0)

def rounded(values):
    return lax.optimization_barrier(values.astype(jnp.bfloat16)).astype(jnp.float32)

def prefill(queries, keys, values):
    score_scale = 1.0 / math.sqrt(HEAD_WIDTH)
    group_size = Q_HEADS // KV_HEADS
    block_size = math.gcd(PROMPT, 512)
    query_heads = queries.reshape(PROMPT, KV_HEADS, group_size, HEAD_WIDTH)
    key_heads = keys.reshape(PROMPT, KV_HEADS, HEAD_WIDTH)
    value_heads = values.reshape(PROMPT, KV_HEADS, HEAD_WIDTH)
    outputs = []
    for row_first in range(0, PROMPT, block_size):
        key_span = row_first + block_size
        query_block = jnp.moveaxis(query_heads[row_first:key_span], 1, 0)
        key_block = jnp.moveaxis(key_heads[:key_span], 1, 0)
        value_block = jnp.moveaxis(value_heads[:key_span], 1, 0)
        query_pos = row_first + jnp.arange(block_size)
        key_pos = jnp.arange(key_span)
        allowed = key_pos[None, :] <= query_pos[:, None]

        def one_head(operands):
            query_one, key_one, value_one = operands
            scores = jnp.einsum('qgd,kd->gqk', query_one.astype(jnp.float32), key_one.astype(jnp.float32)) * score_scale
            scores = jnp.where(allowed[None], scores, -jnp.inf)
            top_row = lax.optimization_barrier(jnp.max(scores, axis=-1, keepdims=True))
            exponent = jnp.exp(scores - top_row)
            weight_sum = lax.optimization_barrier(jnp.sum(exponent, axis=-1))
            attention_weights = rounded(exponent)
            result = jnp.einsum('gqk,kd->gqd', attention_weights, value_one.astype(jnp.float32)) / weight_sum[..., None]
            return jnp.moveaxis(result, 0, 1)
        head_out = lax.map(one_head, (query_block, key_block, value_block))
        outputs.append(jnp.moveaxis(head_out, 0, 1).reshape(block_size, Q_HEADS * HEAD_WIDTH).astype(jnp.bfloat16))
    return jnp.concatenate(outputs, axis=0)

def decode(dec_q, dec_k, dec_v, keys, values):
    score_scale = 1.0 / math.sqrt(HEAD_WIDTH)
    group_size = Q_HEADS // KV_HEADS
    blocks = SAMPLES // SAMPLES_PER_REP
    prompt_keys = jnp.moveaxis(keys.reshape(PROMPT, KV_HEADS, HEAD_WIDTH), 1, 0)
    prompt_values = jnp.moveaxis(values.reshape(PROMPT, KV_HEADS, HEAD_WIDTH), 1, 0)
    step_pos = jnp.arange(STEPS)
    allowed = step_pos[None, :] <= step_pos[:, None]
    query_all = dec_q.reshape(blocks, SAMPLES_PER_REP, STEPS, KV_HEADS, group_size, HEAD_WIDTH)
    key_all = dec_k.reshape(blocks, SAMPLES_PER_REP, STEPS, KV_HEADS, HEAD_WIDTH)
    value_all = dec_v.reshape(blocks, SAMPLES_PER_REP, STEPS, KV_HEADS, HEAD_WIDTH)

    def one_block(operands):
        query_block, key_block, value_block = operands

        def one_head(head_operands):
            query_one, suffix_keys, suffix_values, single_keys, single_values = head_operands
            query_f = query_one.astype(jnp.float32)
            prefix_scores = jnp.einsum('njgd,bd->gnjb', query_f, single_keys.astype(jnp.float32)) * score_scale
            suffix_scores = jnp.einsum('njgd,nud->gnju', query_f, suffix_keys.astype(jnp.float32)) * score_scale
            suffix_scores = jnp.where(allowed[None, None], suffix_scores, -jnp.inf)
            top_row = jnp.maximum(lax.optimization_barrier(jnp.max(prefix_scores, axis=-1)), lax.optimization_barrier(jnp.max(suffix_scores, axis=-1)))
            prefix_exp = jnp.exp(prefix_scores - top_row[..., None])
            suffix_exp = jnp.exp(suffix_scores - top_row[..., None])
            weight_sum = lax.optimization_barrier(jnp.sum(prefix_exp, axis=-1)) + lax.optimization_barrier(jnp.sum(suffix_exp, axis=-1))
            mixed = jnp.einsum('gnjb,bd->gnjd', rounded(prefix_exp), single_values.astype(jnp.float32))
            mixed = mixed + jnp.einsum('gnju,nud->gnjd', rounded(suffix_exp), suffix_values.astype(jnp.float32))
            return mixed / weight_sum[..., None]
        head_out = lax.map(one_head, (jnp.moveaxis(query_block, 2, 0), jnp.moveaxis(key_block, 2, 0), jnp.moveaxis(value_block, 2, 0), prompt_keys, prompt_values))
        head_out = jnp.transpose(head_out, (2, 3, 0, 1, 4))
        return head_out.reshape(SAMPLES_PER_REP, STEPS, Q_HEADS * HEAD_WIDTH).astype(jnp.bfloat16)
    result = lax.map(one_block, (query_all, key_all, value_all))
    return result.reshape(SAMPLES, STEPS, Q_HEADS * HEAD_WIDTH)

def reference(prompt_q, prompt_k, prompt_v, dec_q, dec_k, dec_v):
    keys = unfold(prompt_k)
    values = unfold(prompt_v)
    prefill_out = refold(prefill(unfold(prompt_q), keys, values))
    decode_out = decode(dec_q, dec_k, dec_v, keys, values)
    return (prefill_out, decode_out)
```

```python
import math

import jax
import jax.numpy as jnp
from jax import lax
from jax.experimental import pallas as pl
from jax.experimental.pallas import tpu as pltpu
from jax.sharding import PartitionSpec as P

WIDTH = 128
MESH = pl.DeviceIdType.MESH
SCALE = math.log2(math.e) / math.sqrt(WIDTH)
LOW = -1e30
NT = (((1,), (1,)), ((), ()))
NX, NY, NZ = 4, 8, 4
TOK = 64
GROUP = 8
HALF = TOK * GROUP
MAIN = 2 * HALF
DEC = 160
ROWS = MAIN + DEC
KEYS = NY * TOK
CUT = ROWS // 2
BLOCK = 128
F32, BF16 = jnp.float32, jnp.bfloat16


def kernel(
    pq, pk, pv, dqkv, out, dout,
    qbuf, kv, acc, top, part, stat, got, gstat, mid, mstat, dgat,
    zs, zr, ys, yr, qs, qr, ms, mr, fs, fr, ds, dr,
):
    rep, y, tp = lax.axis_index("rep"), lax.axis_index("seq"), lax.axis_index("tp")
    z, x = rep // NX, rep % NX

    def at(zz, xx, yy):
        return (zz * NX + xx, yy, tp)

    right, left = at(z, (x + 1) % NX, y), at(z, (x + NX - 1) % NX, y)
    ynext, yprev = at(z, x, (y + 1) % NY), at(z, x, (y + NY - 1) % NY)
    stacked = [at((z + j) % NZ, x, y) for j in range(1, NZ)]
    peers = (right, left, ynext, yprev, *stacked)

    def send(src, dst, ssem, rsem, dev):
        return pltpu.make_async_remote_copy(
            src_ref=src, dst_ref=dst, send_sem=ssem, recv_sem=rsem, device_id=dev, device_id_type=MESH
        )

    barrier = pltpu.get_barrier_semaphore()
    for dev in peers:
        pl.semaphore_signal(barrier, inc=1, device_id=dev, device_id_type=MESH)

    kv[z, :, 0:TOK, 0:WIDTH] = pk[...]
    kv[z, :, 0:TOK, WIDTH : 2 * WIDTH] = pv[...]
    for half in range(2):
        for g in range(GROUP):
            qbuf[0, half * HALF + g * TOK : half * HALF + (g + 1) * TOK, :] = pq[
                half, :, g * WIDTH : (g + 1) * WIDTH
            ]
    qbuf[0, MAIN:ROWS, :] = dqkv[0]

    pl.semaphore_wait(barrier, len(peers))

    planes = (
        z,
        jnp.where(z == 0, 1, z - 1),
        jnp.where(z < 2, 2, jnp.where(z == 2, 3, 1)),
        jnp.where(z < 2, 3, 0),
    )

    def plane_at(k):
        return jnp.where(k == 0, planes[0], jnp.where(k == 1, planes[1], jnp.where(k == 2, planes[2], planes[3])))

    def slot(p, r):
        return kv.at[p, :, pl.ds(r * TOK, TOK), :]

    def slot_half(p, r, half):
        return kv.at[p, half, pl.ds(r * TOK, TOK), :]

    def z_copy(j):
        own = slot(z, 0)
        return send(own, own, zs.at[j - 1], zr.at[z], stacked[j - 1])

    def z_arrive(p):
        here = slot(p, 0)
        send(here, here, zs.at[0], zr.at[p], right).wait_recv()

    def y_copies(p, d):
        if d == 1:
            a, b = slot(p, 0), slot(p, 0)
        else:
            a, b = slot(p, 2 * d - 3), slot(p, 2 * d - 2)
        if d < 4:
            return (
                send(a, slot(p, 2 * d - 1), ys.at[p, 2 * d - 2], yr.at[p, 2 * d - 2], ynext),
                send(b, slot(p, 2 * d), ys.at[p, 2 * d - 1], yr.at[p, 2 * d - 1], yprev),
            )
        return (
            send(slot_half(p, 5, 0), slot_half(p, 7, 0), ys.at[p, 6], yr.at[p, 6], ynext),
            send(slot_half(p, 6, 1), slot_half(p, 7, 1), ys.at[p, 7], yr.at[p, 7], yprev),
        )

    def z_step(k):
        if k == 0:
            for j in range(1, NZ):
                z_copy(j).start()
        else:
            z_arrive(planes[k])
        for copy in y_copies(planes[k], 1):
            copy.start()

    def y_step(k, d):
        p = planes[k]
        for copy in y_copies(p, d):
            copy.wait_recv()
        if d < 4:
            for copy in y_copies(p, d + 1):
                copy.start()

    first, second = pl.ds(0, CUT), pl.ds(CUT, CUT)

    def q_copy(i):
        src, dst, rows, dev = (
            (0, 1, first, right),
            (0, 3, second, left),
            (0, 1, second, right),
            (0, 3, first, left),
            (1, 2, first, right),
            (3, 2, second, left),
        )[i]
        return send(qbuf.at[src, rows, :], qbuf.at[dst, rows, :], qs.at[i], qr.at[i], dev)

    def q_forward():
        q_copy(0).wait_recv()
        q_copy(4).start()
        q_copy(1).wait_recv()
        q_copy(5).start()

    def values(p, half):
        v = kv[p, half, :, WIDTH : 2 * WIDTH]
        return kv[p, half, :, 0:WIDTH], jnp.concatenate([v, jnp.ones_like(v)], axis=1)

    def update(s, r0, n, keys, vals, allowed=None):
        rows = pl.ds(r0, n)
        scores = lax.dot_general(qbuf[s, rows, :], keys, NT, preferred_element_type=F32)
        if allowed is not None:
            scores = jnp.where(allowed, scores, LOW)
        top_old = top[s, rows, :]
        top_new = jnp.maximum(top_old, jnp.max(scores, axis=-1, keepdims=True) * SCALE)
        shrink = jnp.exp2(top_old - top_new)
        span = scores.shape[1]
        anchor = top_new[:, 0:1] if span % WIDTH else jnp.tile(top_new, (1, span // WIDTH))
        weights = jnp.exp2(scores * SCALE - anchor).astype(BF16)
        top[s, rows, :] = top_new
        acc[s, rows, :] = acc[s, rows, :] * jnp.concatenate([shrink, shrink], axis=1) + jnp.dot(
            weights, vals, preferred_element_type=F32
        )

    def main_rows(s, p, h, lo, hi):
        k0, v0 = values(p, 0)
        for j in range(lo, hi):
            update(s, HALF + j * BLOCK, BLOCK, k0, v0)
        kh, vh = values(p, h)
        for j in range(lo, hi):
            update(s, pl.multiple_of(h * HALF + j * BLOCK, BLOCK), BLOCK, kh, vh)

    def dec_rows(s, p):
        for half in range(2):
            kk, vv = values(p, half)
            update(s, MAIN, DEC, kk, vv)

    def which(s, k, p):
        far = (x + jnp.where(s == 1, 3, jnp.where(s == 3, 1, 2))) % NX
        return jnp.where(k == 0, jnp.where(x < far, 0, 1), jnp.where(p < z, 0, 1))

    def eye(n):
        return lax.broadcasted_iota(jnp.int32, (n, WIDTH), 0) == lax.broadcasted_iota(jnp.int32, (n, WIDTH), 1)

    def finish(s, r0, n, target, starget, row, count):
        rows = pl.ds(r0, n)
        total = acc[s, rows, WIDTH : 2 * WIDTH]
        target[rows, :] = (acc[s, rows, 0:WIDTH] / jnp.maximum(total, 1e-30)).astype(BF16)
        mask = eye(n)
        starget[row : row + 1, :] = jnp.sum(jnp.where(mask, top[s, rows, :], 0.0), axis=0, keepdims=True)
        starget[row + count : row + count + 1, :] = jnp.sum(jnp.where(mask, total, 0.0), axis=0, keepdims=True)

    def merge(s, r0, n, source, ssource, row, count):
        rows = pl.ds(r0, n)
        mask = eye(n)

        def column(r):
            return jnp.sum(jnp.where(mask, ssource[r : r + 1, :], 0.0), axis=1, keepdims=True)

        top_in, sum_in = column(row), column(row + count)
        top_old = top[s, rows, :]
        top_new = jnp.maximum(top_old, top_in)
        shrink = jnp.exp2(top_old - top_new)
        gain = jnp.exp2(top_in - top_new) * sum_in
        top[s, rows, :] = top_new
        acc[s, rows, 0:WIDTH] = acc[s, rows, 0:WIDTH] * shrink + source[rows, :].astype(F32) * gain
        acc[s, rows, WIDTH : 2 * WIDTH] = acc[s, rows, WIDTH : 2 * WIDTH] * shrink + gain

    def section(c):
        if c < 2:
            return [(c * HALF + j * BLOCK, BLOCK, j) for j in range(4)], 4, c * HALF, HALF
        first_row = MAIN + (c - 2) * (DEC // 2)
        return [(first_row, DEC // 2, 0)], 1, first_row, DEC // 2

    def finish_section(s, c):
        blocks, count, _, _ = section(c)
        for r0, n, j in blocks:
            finish(s, r0, n, part.at[s], stat.at[s, c], j, count)

    def merge_section(s, c, source, ssource):
        blocks, count, _, _ = section(c)
        for r0, n, j in blocks:
            merge(s, r0, n, source, ssource.at[c], j, count)

    def relay_copies(c):
        _, _, r0, n = section(c)
        rows, dev = pl.ds(r0, n), (right, left)[c % 2]
        return (
            send(part.at[2, rows, :], mid.at[rows, :], ms.at[c], mr.at[c], dev),
            send(stat.at[2, c], mstat.at[c], ms.at[4 + c], mr.at[4 + c], dev),
        )

    def final_copies(s, c):
        _, _, r0, n = section(c)
        rows, side = pl.ds(r0, n), 0 if s == 1 else 1
        dev, i = (left, right)[side], 4 * side + c
        return (
            send(part.at[s, rows, :], got.at[side, rows, :], fs.at[i], fr.at[i], dev),
            send(stat.at[s, c], gstat.at[side, c], fs.at[8 + i], fr.at[8 + i], dev),
        )

    def start(copies):
        for copy in copies:
            copy.start()

    def arrive(copies):
        for copy in copies:
            copy.wait_recv()

    def take_relay(c):
        arrive(relay_copies(c))
        merge_section((3, 1)[c % 2], c, mid, mstat)

    def take_final(c):
        for s in (1, 3):
            arrive(final_copies(s, c))
        for side in range(2):
            merge_section(0, c, got.at[side], gstat.at[side])

    def d_copies(d):
        if d == 1:
            a, b = 0, 0
        else:
            a, b = 2 * d - 3, 2 * d - 2
        if d < 4:
            return (
                send(dgat.at[a], dgat.at[2 * d - 1], ds.at[2 * d - 2], dr.at[2 * d - 2], ynext),
                send(dgat.at[b], dgat.at[2 * d], ds.at[2 * d - 1], dr.at[2 * d - 1], yprev),
            )
        top_rows, low_rows = pl.ds(0, DEC // 2), pl.ds(DEC // 2, DEC // 2)
        return (
            send(dgat.at[5, top_rows, :], dgat.at[7, top_rows, :], ds.at[6], dr.at[6], ynext),
            send(dgat.at[6, low_rows, :], dgat.at[7, low_rows, :], ds.at[7], dr.at[7], yprev),
        )

    def place(r):
        delta = -(r + 1) // 2 if r % 2 else r // 2
        column = pl.multiple_of(((y + delta + NY) % NY) * WIDTH, WIDTH)
        dout[:, pl.ds(column, WIDTH)] = dgat[r]

    def d_step(d):
        arrive(d_copies(d))
        if d < 4:
            start(d_copies(d + 1))
            place(2 * d - 1)
            place(2 * d)
        else:
            place(7)

    z_step(0)
    for i in range(4):
        q_copy(i).start()

    for s in range(4):
        acc[s] = jnp.zeros((ROWS, 2 * WIDTH), F32)
        top[s] = jnp.full((ROWS, WIDTH), LOW, F32)

    step_row = lax.broadcasted_iota(jnp.int32, (DEC, DEC), 0)
    step_col = lax.broadcasted_iota(jnp.int32, (DEC, DEC), 1)
    own_v = dqkv[2]
    update(
        0, MAIN, DEC, dqkv[1], jnp.concatenate([own_v, jnp.ones_like(own_v)], axis=1),
        (step_row // 4 == step_col // 4) & (step_col <= step_row),
    )

    y_step(0, 1)
    z_step(1)
    y_step(0, 2)
    y_step(1, 1)
    z_step(2)
    q_forward()
    y_step(0, 3)
    y_step(1, 2)
    y_step(0, 4)

    p0 = planes[0]
    key_col = lax.broadcasted_iota(jnp.int32, (BLOCK, KEYS), 1)
    key_slot = key_col // TOK
    key_delta = jnp.where(key_slot % 2 == 1, NY - (key_slot + 1) // 2, key_slot // 2)
    key_index = ((y + key_delta) % NY) * TOK + key_col % TOK
    query_index = y * TOK + lax.broadcasted_iota(jnp.int32, (BLOCK, KEYS), 0) % TOK
    for half in range(2):
        kk, vv = values(p0, half)
        allowed = key_index <= query_index if half == 0 else key_index >= query_index
        for j in range(4):
            update(0, half * HALF + j * BLOCK, BLOCK, kk, vv, allowed)
    y_step(1, 3)
    k0, v0 = values(p0, 0)
    for j in range(4):
        update(0, HALF + j * BLOCK, BLOCK, k0, v0)
    dec_rows(0, p0)
    y_step(2, 1)

    unit_rows = (0, 1, 3, 2, 0, 1, 3, 2, 2, 1, 2, 1, 3, 3, 0, 0)
    unit_plane = (0, 0, 0, 0, 1, 1, 1, 1, 2, 2, 3, 3, 2, 3, 2, 3)

    def lookup(table, t):
        value = jnp.int32(table[0])
        for i in range(1, len(table)):
            value = jnp.where(t == i, table[i], value)
        return value

    def send_finished(s, *sections):
        for c in sections:
            finish_section(s, c)
            start(relay_copies(c) if s == 2 else final_copies(s, c))

    def sampled_last():
        def one(i, carry):
            dec_rows(i // 2, plane_at(2 + i % 2))
            return carry

        lax.fori_loop(0, 8, one, 0)
        send_finished(2, 2, 3)

    def sampled_relay():
        take_relay(2)
        take_relay(3)
        send_finished(1, 2, 3)
        send_finished(3, 2, 3)

    def sampled_out():
        take_final(2)
        take_final(3)
        rows = pl.ds(MAIN, DEC)
        dgat[0] = (acc[0, rows, 0:WIDTH] / acc[0, rows, WIDTH : 2 * WIDTH]).astype(BF16)
        start(d_copies(1))
        place(0)

    def left_relay():
        take_relay(1)
        send_finished(1, 1)

    def right_done():
        send_finished(3, 1)
        take_relay(0)
        send_finished(3, 0)
        d_step(1)

    middle = {
        1: lambda: y_step(1, 4),
        2: lambda: y_step(2, 2),
        3: lambda: y_step(2, 3),
        4: lambda: y_step(3, 2),
        5: lambda: y_step(2, 4),
        6: lambda: y_step(3, 3),
        8: lambda: y_step(3, 4),
        11: sampled_relay,
        12: left_relay,
        14: lambda: d_step(2),
        15: lambda: d_step(4),
    }
    after = {
        1: lambda: z_step(3),
        2: lambda: y_step(3, 1),
        9: sampled_last,
        10: lambda: send_finished(2, 0, 1),
        11: lambda: send_finished(1, 0),
        12: sampled_out,
        13: right_done,
        14: lambda: d_step(3),
    }
    before = {
        1: lambda: q_copy(2).wait_recv(),
        2: lambda: q_copy(3).wait_recv(),
        3: lambda: (q_copy(4).wait_recv(), q_copy(5).wait_recv())[0],
    }

    def hook(table, t):
        for i, step in table.items():
            pl.when(t == i)(step)

    def unit(t, carry):
        hook(before, t)
        k, s = lookup(unit_plane, t), lookup(unit_rows, t)
        p = plane_at(k)
        h = which(s, k, p)
        main_rows(s, p, h, 0, 2)
        hook(middle, t)
        main_rows(s, p, h, 2, 4)
        pl.when(t < 8)(lambda: dec_rows(s, p))
        hook(after, t)
        return carry

    lax.fori_loop(1, 16, unit, 0)
    for c in (0, 1):
        take_final(c)
        for g in range(GROUP):
            rows = pl.ds(c * HALF + g * TOK, TOK)
            out[c, :, g * WIDTH : (g + 1) * WIDTH] = (
                acc[0, rows, 0:WIDTH] / acc[0, rows, WIDTH : 2 * WIDTH]
            ).astype(BF16)

    for j in range(1, NZ):
        z_copy(j).wait_send()
    for p in range(NZ):
        for d in range(1, 5):
            for copy in y_copies(p, d):
                copy.wait_send()
    for i in range(6):
        q_copy(i).wait_send()
    for c in range(4):
        for copy in (*relay_copies(c), *final_copies(1, c), *final_copies(3, c), *d_copies(c + 1)):
            copy.wait_send()


def local(prompt_q, prompt_k, prompt_v, dec_q, dec_k, dec_v):
    head = lax.axis_index("seq") * WIDTH
    mine = lax.dynamic_slice_in_dim(dec_q, head, WIDTH, 2)
    dqkv = jnp.stack([mine, dec_k, dec_v]).reshape(3, DEC, WIDTH)
    vmem = pl.BlockSpec(memory_space=pltpu.VMEM)
    dma = pltpu.SemaphoreType.DMA
    prefill_out, decode_out = pl.pallas_call(
        kernel,
        out_shape=(
            jax.ShapeDtypeStruct((2, TOK, GROUP * WIDTH), BF16),
            jax.ShapeDtypeStruct((DEC, GROUP * WIDTH), BF16),
        ),
        in_specs=[vmem] * 4,
        out_specs=(vmem, vmem),
        scratch_shapes=[
            pltpu.VMEM((4, ROWS, WIDTH), BF16),
            pltpu.VMEM((NZ, 2, KEYS, 2 * WIDTH), BF16),
            pltpu.VMEM((4, ROWS, 2 * WIDTH), F32),
            pltpu.VMEM((4, ROWS, WIDTH), F32),
            pltpu.VMEM((4, ROWS, WIDTH), BF16),
            pltpu.VMEM((4, 4, 8, WIDTH), F32),
            pltpu.VMEM((2, ROWS, WIDTH), BF16),
            pltpu.VMEM((2, 4, 8, WIDTH), F32),
            pltpu.VMEM((ROWS, WIDTH), BF16),
            pltpu.VMEM((4, 8, WIDTH), F32),
            pltpu.VMEM((8, DEC, WIDTH), BF16),
            dma((NZ,)),
            dma((NZ,)),
            dma((NZ, 8)),
            dma((NZ, 8)),
            dma((6,)),
            dma((6,)),
            dma((8,)),
            dma((8,)),
            dma((16,)),
            dma((16,)),
            dma((8,)),
            dma((8,)),
        ],
        compiler_params=pltpu.CompilerParams(
            collective_id=0, has_side_effects=True, vmem_limit_bytes=48 << 20
        ),
    )(prompt_q, prompt_k, prompt_v, dqkv)
    return prefill_out, decode_out.reshape(dec_q.shape)


def solution(mesh):
    placed = (
        P(None, ("rep", "seq"), "tp"),
        P(None, ("rep", "seq"), "tp"),
        P(None, ("rep", "seq"), "tp"),
        P("rep", None, "tp"),
        P("rep", None, "tp"),
        P("rep", None, "tp"),
    )
    return jax.shard_map(
        local,
        mesh=mesh,
        in_specs=placed,
        out_specs=(P(None, ("rep", "seq"), "tp"), P("rep", None, "tp")),
        check_vma=False,
    )
```

```python
import math

import jax
import jax.numpy as jnp
from jax import lax
from jax.experimental import pallas as pl
from jax.experimental.pallas import tpu as pltpu
from jax.sharding import PartitionSpec as P

WIDTH = 128
MESH = pl.DeviceIdType.MESH
SCALE = math.log2(math.e) / math.sqrt(WIDTH)
LOW = -1e30
NT = (((1,), (1,)), ((), ()))
NX, NY, NZ = 4, 8, 4
TOK = 64
GROUP = 8
HALF = TOK * GROUP
MAIN = 2 * HALF
DEC = 160
ROWS = MAIN + DEC
KEYS = NY * TOK
BLOCK = 128
PART = KEYS // 2
F32, BF16 = jnp.float32, jnp.bfloat16


def kernel(
    pq, pk, pv, dqkv, out, dout,
    qbuf, kv, acc, top, part, stat, got, gstat, dgat,
    zs, zr, ys, yr, qs, qr, fs, fr, ds, dr,
):
    rep, y, tp = lax.axis_index("rep"), lax.axis_index("seq"), lax.axis_index("tp")
    z, x = rep // NX, rep % NX

    def at(zz, xx, yy):
        return (zz * NX + xx, yy, tp)

    along_x = [at(z, (x + j) % NX, y) for j in range(NX)]
    along_y = [at(z, x, (y + j) % NY) for j in range(NY)]
    along_z = [at((z + j) % NZ, x, y) for j in range(NZ)]
    peers = along_x[1:] + along_y[1:] + along_z[1:]

    def send(src, dst, ssem, rsem, dev):
        return pltpu.make_async_remote_copy(
            src_ref=src, dst_ref=dst, send_sem=ssem, recv_sem=rsem, device_id=dev, device_id_type=MESH
        )

    def start(copies):
        for copy in copies:
            copy.start()

    def arrive(copies):
        for copy in copies:
            copy.wait_recv()

    barrier = pltpu.get_barrier_semaphore()
    for dev in peers:
        pl.semaphore_signal(barrier, inc=1, device_id=dev, device_id_type=MESH)

    kv[z, :, 0, 0:TOK, 0:WIDTH] = pk[...]
    kv[z, :, 0, 0:TOK, WIDTH : 2 * WIDTH] = pv[...]
    for half in range(2):
        for g in range(GROUP):
            qbuf[0, half * HALF + g * TOK : half * HALF + (g + 1) * TOK, :] = pq[
                half, :, g * WIDTH : (g + 1) * WIDTH
            ]
    qbuf[0, MAIN:ROWS, :] = dqkv[0]

    pl.semaphore_wait(barrier, len(peers))

    planes = (
        z,
        jnp.where(z == 0, 1, z - 1),
        jnp.where(z < 2, 2, jnp.where(z == 2, 3, 1)),
        jnp.where(z < 2, 3, 0),
    )

    def plane_at(k):
        return jnp.where(k == 0, planes[0], jnp.where(k == 1, planes[1], jnp.where(k == 2, planes[2], planes[3])))

    def slot(p, r):
        return kv.at[p, :, r // 4, pl.ds(r % 4 * TOK, TOK), :]

    def slot_half(p, r, half):
        return kv.at[p, half, r // 4, pl.ds(r % 4 * TOK, TOK), :]

    def z_copy(j):
        own = slot(z, 0)
        return send(own, own, zs.at[j - 1], zr.at[z], along_z[j])

    def z_arrive(p):
        here = slot(p, 0)
        send(here, here, zs.at[0], zr.at[p], along_z[1]).wait_recv()

    def ring_copies(p, d):
        a, b = (0, 0) if d == 1 else (2 * d - 3, 2 * d - 2)
        if d < 4:
            pairs = (slot(p, a), slot(p, 2 * d - 1)), (slot(p, b), slot(p, 2 * d))
        else:
            pairs = (slot_half(p, a, 0), slot_half(p, 7, 0)), (slot_half(p, b, 1), slot_half(p, 7, 1))
        return [
            send(*pair, ys.at[p, 2 * d - 2 + i], yr.at[p, 2 * d - 2 + i], along_y[1 - 2 * i])
            for i, pair in enumerate(pairs)
        ]

    def steps(k):
        return [ring_copies(planes[k], d) for d in range(1, 5)]

    def z_step(k):
        if k == 0:
            for j in range(1, NZ):
                z_copy(j).start()
        else:
            z_arrive(planes[k])
        start(steps(k)[0])

    def y_step(k, d):
        arrive(steps(k)[d - 1])
        if d < len(steps(k)):
            start(steps(k)[d])

    def q_copy(j):
        return send(qbuf.at[0], qbuf.at[j], qs.at[j - 1], qr.at[j - 1], along_x[j])

    def values(half, *items):
        def columns(first):
            parts = [kv[p, half, group, :, first : first + WIDTH] for p, group in items]
            return parts[0] if len(parts) == 1 else jnp.concatenate(parts, axis=0)

        v = columns(WIDTH)
        return columns(0), jnp.concatenate([v, jnp.ones_like(v)], axis=1)

    def update(s, r0, n, keys, vals, allowed=None):
        rows = pl.ds(r0, n)
        scores = lax.dot_general(qbuf[s, rows, :], keys, NT, preferred_element_type=F32)
        if allowed is not None:
            scores = jnp.where(allowed, scores, LOW)
        top_old = top[s, rows, :]
        top_new = jnp.maximum(top_old, jnp.max(scores, axis=-1, keepdims=True) * SCALE)
        shrink = jnp.exp2(top_old - top_new)
        span = scores.shape[1]
        anchor = top_new[:, 0:1] if span % WIDTH else jnp.tile(top_new, (1, span // WIDTH))
        weights = jnp.exp2(scores * SCALE - anchor).astype(BF16)
        top[s, rows, :] = top_new
        acc[s, rows, :] = acc[s, rows, :] * jnp.concatenate([shrink, shrink], axis=1) + jnp.dot(
            weights, vals, preferred_element_type=F32
        )

    def main_rows(s, items, halves):
        k0, v0 = values(0, *items)
        for j in range(HALF // BLOCK):
            update(s, HALF + j * BLOCK, BLOCK, k0, v0)
        for item, h in zip(items, halves):
            kh, vh = values(h, item)
            for j in range(HALF // BLOCK):
                update(s, pl.multiple_of(h * HALF + j * BLOCK, BLOCK), BLOCK, kh, vh)

    def sampled(item, carry):
        for half in range(2):
            kk, vv = values(half, (plane_at(item % NZ), item // NZ))
            for s in range(4):
                update(s, MAIN, DEC, kk, vv)
        return carry

    def which(s, k, p):
        far = (x + NX - s) % NX
        return jnp.where(k == 0, jnp.where(x < far, 0, 1), jnp.where(p < z, 0, 1))

    def eye(n):
        return lax.broadcasted_iota(jnp.int32, (n, WIDTH), 0) == lax.broadcasted_iota(jnp.int32, (n, WIDTH), 1)

    def finish(s, r0, n, target, starget, row, count):
        rows = pl.ds(r0, n)
        total = acc[s, rows, WIDTH : 2 * WIDTH]
        target[rows, :] = (acc[s, rows, 0:WIDTH] / jnp.maximum(total, 1e-30)).astype(BF16)
        mask = eye(n)
        starget[row : row + 1, :] = jnp.sum(jnp.where(mask, top[s, rows, :], 0.0), axis=0, keepdims=True)
        starget[row + count : row + count + 1, :] = jnp.sum(jnp.where(mask, total, 0.0), axis=0, keepdims=True)

    def merge(s, r0, n, source, ssource, row, count):
        rows = pl.ds(r0, n)
        mask = eye(n)

        def column(r):
            return jnp.sum(jnp.where(mask, ssource[r : r + 1, :], 0.0), axis=1, keepdims=True)

        top_in, sum_in = column(row), column(row + count)
        top_old = top[s, rows, :]
        top_new = jnp.maximum(top_old, top_in)
        shrink = jnp.exp2(top_old - top_new)
        gain = jnp.exp2(top_in - top_new) * sum_in
        top[s, rows, :] = top_new
        acc[s, rows, 0:WIDTH] = acc[s, rows, 0:WIDTH] * shrink + source[rows, :].astype(F32) * gain
        acc[s, rows, WIDTH : 2 * WIDTH] = acc[s, rows, WIDTH : 2 * WIDTH] * shrink + gain

    def section(c):
        if c < 2:
            return [(c * HALF + j * BLOCK, BLOCK, c, j) for j in range(4)], 4, pl.ds(c * HALF, HALF), pl.ds(c, 1)
        half = DEC // 2
        return [(MAIN + j * half, half, 2 + j, 0) for j in range(2)], 1, pl.ds(MAIN, DEC), pl.ds(2, 2)

    def final_copies(s, c):
        _, _, rows, sheets = section(c)
        i, owner = 3 * (s - 1) + c, at(z, (x + NX - s) % NX, y)
        return [
            send(part.at[s, rows, :], got.at[s - 1, rows, :], fs.at[i], fr.at[i], owner),
            send(stat.at[s, sheets], gstat.at[s - 1, sheets], fs.at[9 + i], fr.at[9 + i], owner),
        ]

    def give(s, c):
        blocks, count, _, _ = section(c)
        for r0, n, sheet, j in blocks:
            finish(s, r0, n, part.at[s], stat.at[s, sheet], j, count)
        start(final_copies(s, c))

    def take(s, c):
        arrive(final_copies(s, c))
        blocks, count, _, _ = section(c)
        for r0, n, sheet, j in blocks:
            merge(0, r0, n, got.at[s - 1], gstat.at[s - 1, sheet], j, count)

    def give_sampled(s, carry):
        give(s, 2)
        return carry

    def take_sampled(s, carry):
        take(s, 2)
        return carry

    def d_copy(j):
        return send(dgat.at[0], dgat.at[j], ds.at[j - 1], dr.at[j - 1], along_y[j])

    def place(j):
        column = pl.multiple_of(((y + NY - j) % NY) * WIDTH, WIDTH)
        dout[:, pl.ds(column, WIDTH)] = dgat[j]

    z_step(0)
    q_copy(1).start()
    q_copy(3).start()

    def clear(s, carry):
        acc[s] = jnp.zeros((ROWS, 2 * WIDTH), F32)
        top[s] = jnp.full((ROWS, WIDTH), LOW, F32)
        return carry

    lax.fori_loop(0, 4, clear, 0)

    step_row = lax.broadcasted_iota(jnp.int32, (DEC, DEC), 0)
    step_col = lax.broadcasted_iota(jnp.int32, (DEC, DEC), 1)
    own_v = dqkv[2]
    update(
        0, MAIN, DEC, dqkv[1], jnp.concatenate([own_v, jnp.ones_like(own_v)], axis=1),
        (step_row // 4 == step_col // 4) & (step_col <= step_row),
    )

    def own_plane(group):
        shape = (BLOCK, PART)
        key = group * PART + lax.broadcasted_iota(jnp.int32, shape, 1)
        key_slot = key // TOK
        key_delta = jnp.where(key_slot % 2 == 1, NY - (key_slot + 1) // 2, key_slot // 2)
        key_index = ((y + key_delta) % NY) * TOK + key % TOK
        query_index = y * TOK + lax.broadcasted_iota(jnp.int32, shape, 0) % TOK
        k0, v0 = values(0, (planes[0], group))
        k1, v1 = values(1, (planes[0], group))
        for j in range(HALF // BLOCK):
            update(0, HALF + j * BLOCK, BLOCK, k0, v0)
            update(0, j * BLOCK, BLOCK, k0, v0, key_index <= query_index)
        for j in range(HALF // BLOCK):
            update(0, HALF + j * BLOCK, BLOCK, k1, v1, key_index >= query_index)

    y_step(0, 1)
    q_copy(2).start()
    for k in range(1, NZ):
        z_step(k)
    for k in range(1, NZ):
        y_step(k, 1)
    y_step(0, 2)

    unit_rows = (0, 1, 3, 2, 0, 1, 3, 2, 2, 1, 2, 1, 3, 3, 0, 0)
    unit_one = (0, 0, 0, 0, 2, 4, 4, 4, 1, 1, 5, 5, 1, 5, 6, 5)
    unit_two = (0, 2, 2, 2, 4, 6, 6, 6, 3, 3, 7, 7, 3, 7, 3, 7)

    def lookup(table, t):
        value = jnp.int32(table[0])
        for i in range(1, len(table)):
            value = jnp.where(t == i, table[i], value)
        return value

    def sampled_out():
        lax.fori_loop(1, NX, take_sampled, 0)
        rows = pl.ds(MAIN, DEC)
        dgat[0] = (acc[0, rows, 0:WIDTH] / acc[0, rows, WIDTH : 2 * WIDTH]).astype(BF16)
        start([d_copy(j) for j in range(1, NY)])
        place(0)

    after = {
        0: [lambda: y_step(1, 2)],
        1: [lambda: y_step(2, 2)],
        2: [lambda: y_step(3, 2)],
        3: [lambda: y_step(0, 3)],
        4: [lambda: y_step(1, 3)],
        5: [lambda: y_step(2, 3)],
        6: [lambda: y_step(3, 3), lambda: y_step(0, 4)],
        7: [lambda: y_step(1, 4)],
        8: [lambda: y_step(2, 4)],
        9: [lambda: y_step(3, 4)],
        12: [sampled_out],
    }
    met = (0, 0, 0, 1, 2, 3, 4, 4, 5, 8, 8, 8, 8, 8, 8, 8)

    before = {
        1: [lambda: q_copy(1).wait_recv()],
        2: [lambda: q_copy(3).wait_recv()],
        3: [lambda: q_copy(2).wait_recv()],
    }

    def hook(table, t):
        for i, work in table.items():

            @pl.when(t == i)
            def _(work=work):
                for step in work:
                    step()

    def unit(t, carry):
        hook(before, t)
        s = lookup(unit_rows, t)

        @pl.when((t == 0) | (t == 8))
        def _():
            own_plane(jnp.where(t == 0, 0, 1))

        @pl.when(t > 0)
        def _():
            items, halves = [], []
            for table in (unit_one, unit_two):
                item = lookup(table, t)
                k, group = item // 2, item % 2
                p = plane_at(k)
                items.append((p, group))
                halves.append(which(s, k, p))
            main_rows(s, items, halves)

        hook(after, t)
        lax.fori_loop(lookup(met, t - 1), lookup(met, t), sampled, 0)

        @pl.when(t == 9)
        def _():
            lax.fori_loop(1, NX, give_sampled, 0)

        @pl.when((t == 10) | (t == 11) | (t == 13))
        def _():
            give(s, 0)
            give(s, 1)

        return carry

    lax.fori_loop(0, 16, unit, 0)

    def take_main(i, carry):
        s = lookup((2, 1, 3), i)
        take(s, 0)
        take(s, 1)
        return carry

    lax.fori_loop(0, 3, take_main, 0)
    for c in range(2):
        for g in range(GROUP):
            rows = pl.ds(c * HALF + g * TOK, TOK)
            out[c, :, g * WIDTH : (g + 1) * WIDTH] = (
                acc[0, rows, 0:WIDTH] / acc[0, rows, WIDTH : 2 * WIDTH]
            ).astype(BF16)
    for j in range(1, NY):
        d_copy(j).wait_recv()
        place(j)

    gone = [z_copy(j) for j in range(1, NZ)] + [q_copy(j) for j in range(1, NX)] + [d_copy(j) for j in range(1, NY)]
    for k in range(NZ):
        for copies in steps(k):
            gone += copies
    for s in range(1, NX):
        for c in range(3):
            gone += final_copies(s, c)
    for copy in gone:
        copy.wait_send()


def local(prompt_q, prompt_k, prompt_v, dec_q, dec_k, dec_v):
    head = lax.axis_index("seq") * WIDTH
    mine = lax.dynamic_slice_in_dim(dec_q, head, WIDTH, 2)
    dqkv = jnp.stack([mine, dec_k, dec_v]).reshape(3, DEC, WIDTH)
    vmem = pl.BlockSpec(memory_space=pltpu.VMEM)
    dma = pltpu.SemaphoreType.DMA
    prefill_out, decode_out = pl.pallas_call(
        kernel,
        out_shape=(
            jax.ShapeDtypeStruct((2, TOK, GROUP * WIDTH), BF16),
            jax.ShapeDtypeStruct((DEC, GROUP * WIDTH), BF16),
        ),
        in_specs=[vmem] * 4,
        out_specs=(vmem, vmem),
        scratch_shapes=[
            pltpu.VMEM((4, ROWS, WIDTH), BF16),
            pltpu.VMEM((NZ, 2, 2, PART, 2 * WIDTH), BF16),
            pltpu.VMEM((4, ROWS, 2 * WIDTH), F32),
            pltpu.VMEM((4, ROWS, WIDTH), F32),
            pltpu.VMEM((4, ROWS, WIDTH), BF16),
            pltpu.VMEM((4, 4, 8, WIDTH), F32),
            pltpu.VMEM((3, ROWS, WIDTH), BF16),
            pltpu.VMEM((3, 4, 8, WIDTH), F32),
            pltpu.VMEM((NY, DEC, WIDTH), BF16),
            dma((NZ - 1,)),
            dma((NZ,)),
            dma((NZ, 8)),
            dma((NZ, 8)),
            dma((NX - 1,)),
            dma((NX - 1,)),
            dma((18,)),
            dma((18,)),
            dma((NY - 1,)),
            dma((NY - 1,)),
        ],
        compiler_params=pltpu.CompilerParams(
            collective_id=0, has_side_effects=True, vmem_limit_bytes=48 << 20
        ),
    )(prompt_q, prompt_k, prompt_v, dqkv)
    return prefill_out, decode_out.reshape(dec_q.shape)


def solution(mesh):
    placed = (
        P(None, ("rep", "seq"), "tp"),
        P(None, ("rep", "seq"), "tp"),
        P(None, ("rep", "seq"), "tp"),
        P("rep", None, "tp"),
        P("rep", None, "tp"),
        P("rep", None, "tp"),
    )
    return jax.shard_map(
        local,
        mesh=mesh,
        in_specs=placed,
        out_specs=(P(None, ("rep", "seq"), "tp"), P("rep", None, "tp")),
        check_vma=False,
    )
```

```python
import math

import jax
import jax.numpy as jnp
from jax import lax
from jax.experimental import pallas as pl
from jax.experimental.pallas import tpu as pltpu
from jax.sharding import PartitionSpec as P

WIDTH = 128
MESH = pl.DeviceIdType.MESH
SCALE = math.log2(math.e) / math.sqrt(WIDTH)
LOW = -1e30
NT = (((1,), (1,)), ((), ()))
NX, NY, NZ = 4, 8, 4
TOK = 64
GROUP = 8
HALF = TOK * GROUP
MAIN = 2 * HALF
DEC = 160
ROWS = MAIN + DEC
KEYS = NY * TOK
BLOCK = 128
PART = KEYS // 2
F32, BF16 = jnp.float32, jnp.bfloat16


def kernel(
    pq, pk, pv, dqkv, out, dout,
    qbuf, kv, acc, top, part, stat, got, gstat, dgat,
    zs, zr, ys, yr, qs, qr, fs, fr, ds, dr,
):
    rep, y, tp = lax.axis_index("rep"), lax.axis_index("seq"), lax.axis_index("tp")
    z, x = rep // NX, rep % NX

    def at(zz, xx, yy):
        return (zz * NX + xx, yy, tp)

    along_x = [at(z, (x + j) % NX, y) for j in range(NX)]
    along_y = [at(z, x, (y + j) % NY) for j in range(NY)]
    along_z = [at((z + j) % NZ, x, y) for j in range(NZ)]
    peers = along_x[1:] + along_y[1:] + along_z[1:]

    def send(src, dst, ssem, rsem, dev):
        return pltpu.make_async_remote_copy(
            src_ref=src, dst_ref=dst, send_sem=ssem, recv_sem=rsem, device_id=dev, device_id_type=MESH
        )

    def start(copies):
        for copy in copies:
            copy.start()

    def arrive(copies):
        for copy in copies:
            copy.wait_recv()

    barrier = pltpu.get_barrier_semaphore()
    for dev in peers:
        pl.semaphore_signal(barrier, inc=1, device_id=dev, device_id_type=MESH)

    kv[z, :, 0, 0:TOK, 0:WIDTH] = pk[...]
    kv[z, :, 0, 0:TOK, WIDTH : 2 * WIDTH] = pv[...]
    for half in range(2):
        for g in range(GROUP):
            qbuf[0, half * HALF + g * TOK : half * HALF + (g + 1) * TOK, :] = pq[
                half, :, g * WIDTH : (g + 1) * WIDTH
            ]
    qbuf[0, MAIN:ROWS, :] = dqkv[0]

    pl.semaphore_wait(barrier, len(peers))

    planes = (
        z,
        jnp.where(z == 0, 1, z - 1),
        jnp.where(z < 2, 2, jnp.where(z == 2, 3, 1)),
        jnp.where(z < 2, 3, 0),
    )

    def plane_at(k):
        return jnp.where(k == 0, planes[0], jnp.where(k == 1, planes[1], jnp.where(k == 2, planes[2], planes[3])))

    def slot(p, r):
        return kv.at[p, :, r // 4, pl.ds(r % 4 * TOK, TOK), :]

    def slot_half(p, r, half):
        return kv.at[p, half, r // 4, pl.ds(r % 4 * TOK, TOK), :]

    def z_copy(i, r=0):
        own = slot(z, r)
        j = (i - 1) + (NZ - 1) * (r > 0)
        return send(own, own, zs.at[j], zr.at[z, int(r > 0)], at(planes[i], x, y))

    def z_arrive(p, r=0):
        here = slot(p, r)
        send(here, here, zs.at[0], zr.at[p, int(r > 0)], along_z[1]).wait_recv()

    def ring_copies(p, d):
        a, b = (0, 0) if d == 1 else (2 * d - 3, 2 * d - 2)
        if d < 4:
            pairs = (slot(p, a), slot(p, 2 * d - 1)), (slot(p, b), slot(p, 2 * d))
        else:
            pairs = (slot_half(p, a, 0), slot_half(p, 7, 0)), (slot_half(p, b, 1), slot_half(p, 7, 1))
        return [
            send(*pair, ys.at[p, 2 * d - 2 + i], yr.at[p, 2 * d - 2 + i], along_y[1 - 2 * i])
            for i, pair in enumerate(pairs)
        ]

    def steps(k):
        return [ring_copies(planes[k], d) for d in range(1, 5 if k == 0 else 4)]

    def z_step(k):
        if k == 0:
            for i in range(1, NZ):
                z_copy(i).start()
        else:
            z_arrive(planes[k])
        start(steps(k)[0])

    def y_step(k, d):
        arrive(steps(k)[d - 1])
        if d < len(steps(k)):
            start(steps(k)[d])
        elif k == 0:
            for i in range(1, NZ):
                z_copy(i, 7).start()

    def far_step(k):
        z_arrive(planes[k], 7)

    def q_copy(j):
        return send(qbuf.at[0], qbuf.at[j], qs.at[j - 1], qr.at[j - 1], along_x[j])

    def values(half, *items):
        def columns(first):
            parts = [kv[p, half, group, :, first : first + WIDTH] for p, group in items]
            return parts[0] if len(parts) == 1 else jnp.concatenate(parts, axis=0)

        v = columns(WIDTH)
        return columns(0), jnp.concatenate([v, jnp.ones_like(v)], axis=1)

    def update(s, r0, n, keys, vals, allowed=None):
        rows = pl.ds(r0, n)
        scores = lax.dot_general(qbuf[s, rows, :], keys, NT, preferred_element_type=F32)
        if allowed is not None:
            scores = jnp.where(allowed, scores, LOW)
        top_old = top[s, rows, :]
        top_new = jnp.maximum(top_old, jnp.max(scores, axis=-1, keepdims=True) * SCALE)
        shrink = jnp.exp2(top_old - top_new)
        span = scores.shape[1]
        anchor = top_new[:, 0:1] if span % WIDTH else jnp.tile(top_new, (1, span // WIDTH))
        weights = jnp.exp2(scores * SCALE - anchor).astype(BF16)
        top[s, rows, :] = top_new
        acc[s, rows, :] = acc[s, rows, :] * jnp.concatenate([shrink, shrink], axis=1) + jnp.dot(
            weights, vals, preferred_element_type=F32
        )

    def main_rows(s, items, halves):
        k0, v0 = values(0, *items)
        for j in range(HALF // BLOCK):
            update(s, HALF + j * BLOCK, BLOCK, k0, v0)
        for item, h in zip(items, halves):
            kh, vh = values(h, item)
            for j in range(HALF // BLOCK):
                update(s, pl.multiple_of(h * HALF + j * BLOCK, BLOCK), BLOCK, kh, vh)

    def sampled(item, carry):
        for half in range(2):
            first = item % 2 * 2
            kk, vv = values(half, (plane_at(first), item // 2), (plane_at(first + 1), item // 2))
            for s in range(4):
                update(s, MAIN, DEC, kk, vv)
        return carry

    def which(s, k, p):
        far = (x + NX - s) % NX
        return jnp.where(k == 0, jnp.where(x < far, 0, 1), jnp.where(p < z, 0, 1))

    def eye(n):
        return lax.broadcasted_iota(jnp.int32, (n, WIDTH), 0) == lax.broadcasted_iota(jnp.int32, (n, WIDTH), 1)

    def finish(s, r0, n, target, starget, row, count):
        rows = pl.ds(r0, n)
        total = acc[s, rows, WIDTH : 2 * WIDTH]
        target[rows, :] = (acc[s, rows, 0:WIDTH] / jnp.maximum(total, 1e-30)).astype(BF16)
        mask = eye(n)
        starget[row : row + 1, :] = jnp.sum(jnp.where(mask, top[s, rows, :], 0.0), axis=0, keepdims=True)
        starget[row + count : row + count + 1, :] = jnp.sum(jnp.where(mask, total, 0.0), axis=0, keepdims=True)

    def merge(s, r0, n, source, ssource, row, count):
        rows = pl.ds(r0, n)
        mask = eye(n)

        def column(r):
            return jnp.sum(jnp.where(mask, ssource[r : r + 1, :], 0.0), axis=1, keepdims=True)

        top_in, sum_in = column(row), column(row + count)
        top_old = top[s, rows, :]
        top_new = jnp.maximum(top_old, top_in)
        shrink = jnp.exp2(top_old - top_new)
        gain = jnp.exp2(top_in - top_new) * sum_in
        top[s, rows, :] = top_new
        acc[s, rows, 0:WIDTH] = acc[s, rows, 0:WIDTH] * shrink + source[rows, :].astype(F32) * gain
        acc[s, rows, WIDTH : 2 * WIDTH] = acc[s, rows, WIDTH : 2 * WIDTH] * shrink + gain

    def section(c):
        if c < 2:
            return [(c * HALF + j * BLOCK, BLOCK, c, j) for j in range(4)], 4, pl.ds(c * HALF, HALF), pl.ds(c, 1)
        half = DEC // 2
        return [(MAIN + j * half, half, 2 + j, 0) for j in range(2)], 1, pl.ds(MAIN, DEC), pl.ds(2, 2)

    def final_copies(s, c):
        _, _, rows, sheets = section(c)
        i, owner = 3 * (s - 1) + c, at(z, (x + NX - s) % NX, y)
        return [
            send(part.at[s, rows, :], got.at[s - 1, rows, :], fs.at[i], fr.at[i], owner),
            send(stat.at[s, sheets], gstat.at[s - 1, sheets], fs.at[9 + i], fr.at[9 + i], owner),
        ]

    def give(s, c):
        blocks, count, _, _ = section(c)
        for r0, n, sheet, j in blocks:
            finish(s, r0, n, part.at[s], stat.at[s, sheet], j, count)
        start(final_copies(s, c))

    def take(s, c):
        arrive(final_copies(s, c))
        blocks, count, _, _ = section(c)
        for r0, n, sheet, j in blocks:
            merge(0, r0, n, got.at[s - 1], gstat.at[s - 1, sheet], j, count)

    def give_sampled(s, carry):
        give(s, 2)
        return carry

    def take_sampled(s, carry):
        take(s, 2)
        return carry

    def d_copy(j):
        return send(dgat.at[0], dgat.at[j], ds.at[j - 1], dr.at[j - 1], along_y[j])

    def place(j):
        column = pl.multiple_of(((y + NY - j) % NY) * WIDTH, WIDTH)
        dout[:, pl.ds(column, WIDTH)] = dgat[j]

    z_step(0)
    q_copy(1).start()
    q_copy(3).start()

    y_step(0, 1)
    z_step(1)

    def clear(s, carry):
        acc[s] = jnp.zeros((ROWS, 2 * WIDTH), F32)
        top[s] = jnp.full((ROWS, WIDTH), LOW, F32)
        return carry

    lax.fori_loop(0, 4, clear, 0)

    step_row = lax.broadcasted_iota(jnp.int32, (DEC, DEC), 0)
    step_col = lax.broadcasted_iota(jnp.int32, (DEC, DEC), 1)
    own_v = dqkv[2]
    update(
        0, MAIN, DEC, dqkv[1], jnp.concatenate([own_v, jnp.ones_like(own_v)], axis=1),
        (step_row // 4 == step_col // 4) & (step_col <= step_row),
    )

    def own_plane(group):
        shape = (BLOCK, PART)
        key = group * PART + lax.broadcasted_iota(jnp.int32, shape, 1)
        key_slot = key // TOK
        key_delta = jnp.where(key_slot % 2 == 1, NY - (key_slot + 1) // 2, key_slot // 2)
        key_index = ((y + key_delta) % NY) * TOK + key % TOK
        query_index = y * TOK + lax.broadcasted_iota(jnp.int32, shape, 0) % TOK
        k0, v0 = values(0, (planes[0], group))
        k1, v1 = values(1, (planes[0], group))
        for j in range(HALF // BLOCK):
            update(0, HALF + j * BLOCK, BLOCK, k0, v0)
            update(0, j * BLOCK, BLOCK, k0, v0, key_index <= query_index)
        for j in range(HALF // BLOCK):
            update(0, HALF + j * BLOCK, BLOCK, k1, v1, key_index >= query_index)

    y_step(0, 2)
    q_copy(2).start()
    z_step(2)
    z_step(3)
    y_step(1, 1)

    unit_rows = (0, 1, 3, 0, 1, 3, 2, 2, 2, 2, 1, 1, 3, 3, 0, 0)
    unit_one = (0, 0, 0, 2, 4, 4, 0, 4, 1, 5, 1, 5, 1, 5, 6, 5)
    unit_two = (0, 2, 2, 4, 6, 6, 2, 6, 3, 7, 3, 7, 3, 7, 3, 7)

    def lookup(table, t):
        value = jnp.int32(table[0])
        for i in range(1, len(table)):
            value = jnp.where(t == i, table[i], value)
        return value

    def sampled_out():
        lax.fori_loop(1, NX, take_sampled, 0)
        rows = pl.ds(MAIN, DEC)
        dgat[0] = (acc[0, rows, 0:WIDTH] / acc[0, rows, WIDTH : 2 * WIDTH]).astype(BF16)
        start([d_copy(j) for j in range(1, NY)])
        place(0)

    after = {
        0: [lambda: y_step(0, 3), lambda: y_step(2, 1), lambda: y_step(3, 1), lambda: y_step(1, 2)],
        1: [lambda: y_step(0, 4), lambda: y_step(2, 2)],
        2: [lambda: y_step(3, 2)],
        3: [lambda: y_step(1, 3)],
        4: [lambda: y_step(2, 3)],
        5: [lambda: y_step(3, 3)],
        7: [lambda: far_step(1)],
        8: [lambda: far_step(2), lambda: far_step(3)],
        11: [sampled_out],
    }
    met = (0, 0, 0, 0, 0, 0, 1, 3, 4, 4, 4, 4, 4, 4, 4, 4)

    before = {
        1: [lambda: q_copy(1).wait_recv()],
        2: [lambda: q_copy(3).wait_recv()],
        6: [lambda: q_copy(2).wait_recv()],
    }

    def hook(table, t):
        for i, work in table.items():

            @pl.when(t == i)
            def _(work=work):
                for step in work:
                    step()

    def unit(t, carry):
        hook(before, t)
        s = lookup(unit_rows, t)

        @pl.when((t == 0) | (t == 8))
        def _():
            own_plane(jnp.where(t == 0, 0, 1))

        @pl.when(t > 0)
        def _():
            items, halves = [], []
            for table in (unit_one, unit_two):
                item = lookup(table, t)
                k, group = item // 2, item % 2
                p = plane_at(k)
                items.append((p, group))
                halves.append(which(s, k, p))
            main_rows(s, items, halves)

        hook(after, t)
        lax.fori_loop(lookup(met, t - 1), lookup(met, t), sampled, 0)

        @pl.when(t == 8)
        def _():
            lax.fori_loop(1, NX, give_sampled, 0)

        @pl.when((t == 9) | (t == 11) | (t == 13))
        def _():
            give(s, 0)
            give(s, 1)

        return carry

    lax.fori_loop(0, 16, unit, 0)

    def take_main(i, carry):
        s = lookup((2, 1, 3), i)
        take(s, 0)
        take(s, 1)
        return carry

    lax.fori_loop(0, 3, take_main, 0)
    for c in range(2):
        for g in range(GROUP):
            rows = pl.ds(c * HALF + g * TOK, TOK)
            out[c, :, g * WIDTH : (g + 1) * WIDTH] = (
                acc[0, rows, 0:WIDTH] / acc[0, rows, WIDTH : 2 * WIDTH]
            ).astype(BF16)
    for j in range(1, NY):
        d_copy(j).wait_recv()
        place(j)

    gone = [z_copy(i, r) for i in range(1, NZ) for r in (0, 7)]
    gone += [q_copy(j) for j in range(1, NX)] + [d_copy(j) for j in range(1, NY)]
    for k in range(NZ):
        for copies in steps(k):
            gone += copies
    for s in range(1, NX):
        for c in range(3):
            gone += final_copies(s, c)
    for copy in gone:
        copy.wait_send()


def local(prompt_q, prompt_k, prompt_v, dec_q, dec_k, dec_v):
    head = lax.axis_index("seq") * WIDTH
    mine = lax.dynamic_slice_in_dim(dec_q, head, WIDTH, 2)
    dqkv = jnp.stack([mine, dec_k, dec_v]).reshape(3, DEC, WIDTH)
    vmem = pl.BlockSpec(memory_space=pltpu.VMEM)
    dma = pltpu.SemaphoreType.DMA
    prefill_out, decode_out = pl.pallas_call(
        kernel,
        out_shape=(
            jax.ShapeDtypeStruct((2, TOK, GROUP * WIDTH), BF16),
            jax.ShapeDtypeStruct((DEC, GROUP * WIDTH), BF16),
        ),
        in_specs=[vmem] * 4,
        out_specs=(vmem, vmem),
        scratch_shapes=[
            pltpu.VMEM((4, ROWS, WIDTH), BF16),
            pltpu.VMEM((NZ, 2, 2, PART, 2 * WIDTH), BF16),
            pltpu.VMEM((4, ROWS, 2 * WIDTH), F32),
            pltpu.VMEM((4, ROWS, WIDTH), F32),
            pltpu.VMEM((4, ROWS, WIDTH), BF16),
            pltpu.VMEM((4, 4, 8, WIDTH), F32),
            pltpu.VMEM((3, ROWS, WIDTH), BF16),
            pltpu.VMEM((3, 4, 8, WIDTH), F32),
            pltpu.VMEM((NY, DEC, WIDTH), BF16),
            dma((2 * NZ - 2,)),
            dma((NZ, 2)),
            dma((NZ, 8)),
            dma((NZ, 8)),
            dma((NX - 1,)),
            dma((NX - 1,)),
            dma((18,)),
            dma((18,)),
            dma((NY - 1,)),
            dma((NY - 1,)),
        ],
        compiler_params=pltpu.CompilerParams(
            collective_id=0, has_side_effects=True, vmem_limit_bytes=48 << 20
        ),
    )(prompt_q, prompt_k, prompt_v, dqkv)
    return prefill_out, decode_out.reshape(dec_q.shape)


def solution(mesh):
    placed = (
        P(None, ("rep", "seq"), "tp"),
        P(None, ("rep", "seq"), "tp"),
        P(None, ("rep", "seq"), "tp"),
        P("rep", None, "tp"),
        P("rep", None, "tp"),
        P("rep", None, "tp"),
    )
    return jax.shard_map(
        local,
        mesh=mesh,
        in_specs=placed,
        out_specs=(P(None, ("rep", "seq"), "tp"), P("rep", None, "tp")),
        check_vma=False,
    )
```

```python
import math

import jax
import jax.numpy as jnp
from jax import lax
from jax.experimental import pallas as pl
from jax.experimental.pallas import tpu as pltpu
from jax.sharding import PartitionSpec as P

WIDTH = 128
MESH = pl.DeviceIdType.MESH
SCALE = math.log2(math.e) / math.sqrt(WIDTH)
LOW = -1e30
NT = (((1,), (1,)), ((), ()))
NX, NY, NZ = 4, 8, 4
TOK = 64
GROUP = 8
HALF = TOK * GROUP
MAIN = 2 * HALF
DEC = 160
ROWS = MAIN + DEC
KEYS = NY * TOK
BLOCK = 128
PART = KEYS // 2
F32, BF16 = jnp.float32, jnp.bfloat16


def kernel(
    pq, pk, pv, dqkv, out, dout,
    qbuf, kv, acc, top, part, stat, got, gstat, dgat,
    zs, zr, ys, yr, qs, qr, fs, fr, ds, dr,
):
    rep, y, tp = lax.axis_index("rep"), lax.axis_index("seq"), lax.axis_index("tp")
    z, x = rep // NX, rep % NX

    def at(zz, xx, yy):
        return (zz * NX + xx, yy, tp)

    along_x = [at(z, (x + j) % NX, y) for j in range(NX)]
    along_y = [at(z, x, (y + j) % NY) for j in range(NY)]
    along_z = [at((z + j) % NZ, x, y) for j in range(NZ)]
    peers = along_x[1:] + along_y[1:] + along_z[1:]

    def send(src, dst, ssem, rsem, dev):
        return pltpu.make_async_remote_copy(
            src_ref=src, dst_ref=dst, send_sem=ssem, recv_sem=rsem, device_id=dev, device_id_type=MESH
        )

    def start(copies):
        for copy in copies:
            copy.start()

    def arrive(copies):
        for copy in copies:
            copy.wait_recv()

    barrier = pltpu.get_barrier_semaphore()
    for dev in peers:
        pl.semaphore_signal(barrier, inc=1, device_id=dev, device_id_type=MESH)

    kv[z, :, 0, 0:TOK, 0:WIDTH] = pk[...]
    kv[z, :, 0, 0:TOK, WIDTH : 2 * WIDTH] = pv[...]
    for half in range(2):
        for g in range(GROUP):
            qbuf[0, half * HALF + g * TOK : half * HALF + (g + 1) * TOK, :] = pq[
                half, :, g * WIDTH : (g + 1) * WIDTH
            ]
    qbuf[0, MAIN:ROWS, :] = dqkv[0]

    pl.semaphore_wait(barrier, len(peers))

    planes = (
        z,
        jnp.where(z == 0, 1, z - 1),
        jnp.where(z < 2, 2, jnp.where(z == 2, 3, 1)),
        jnp.where(z < 2, 3, 0),
    )

    def plane_at(k):
        return jnp.where(k == 0, planes[0], jnp.where(k == 1, planes[1], jnp.where(k == 2, planes[2], planes[3])))

    def slot(p, r):
        return kv.at[p, :, r // 4, pl.ds(r % 4 * TOK, TOK), :]

    def slot_half(p, r, half):
        return kv.at[p, half, r // 4, pl.ds(r % 4 * TOK, TOK), :]

    def z_copy(i, r=0):
        own = slot(z, r)
        j = (i - 1) + (NZ - 1) * (r > 0)
        return send(own, own, zs.at[j], zr.at[z, int(r > 0)], at(planes[i], x, y))

    def z_arrive(p, r=0):
        here = slot(p, r)
        send(here, here, zs.at[0], zr.at[p, int(r > 0)], along_z[1]).wait_recv()

    def ring_copies(p, d):
        a, b = (0, 0) if d == 1 else (2 * d - 3, 2 * d - 2)
        if d < 4:
            pairs = (slot(p, a), slot(p, 2 * d - 1)), (slot(p, b), slot(p, 2 * d))
        else:
            pairs = (slot_half(p, a, 0), slot_half(p, 7, 0)), (slot_half(p, b, 1), slot_half(p, 7, 1))
        return [
            send(*pair, ys.at[p, 2 * d - 2 + i], yr.at[p, 2 * d - 2 + i], along_y[1 - 2 * i])
            for i, pair in enumerate(pairs)
        ]

    def steps(k):
        return [ring_copies(planes[k], d) for d in range(1, 5 if k == 0 else 4)]

    def z_step(k):
        if k == 0:
            for i in range(1, NZ):
                z_copy(i).start()
        else:
            z_arrive(planes[k])
        start(steps(k)[0])

    def y_step(k, d):
        arrive(steps(k)[d - 1])
        if d < len(steps(k)):
            start(steps(k)[d])
        elif k == 0:
            for i in range(1, NZ):
                z_copy(i, 7).start()

    def far_step(k):
        z_arrive(planes[k], 7)

    def q_copy(j):
        return send(qbuf.at[0], qbuf.at[j], qs.at[j - 1], qr.at[j - 1], along_x[j])

    def values(half, *items):
        def columns(first):
            parts = [kv[p, half, group, :, first : first + WIDTH] for p, group in items]
            return parts[0] if len(parts) == 1 else jnp.concatenate(parts, axis=0)

        v = columns(WIDTH)
        return columns(0), jnp.concatenate([v, jnp.ones_like(v)], axis=1)

    def update(s, r0, n, keys, vals, allowed=None):
        rows = pl.ds(r0, n)
        scores = lax.dot_general(qbuf[s, rows, :], keys, NT, preferred_element_type=F32)
        if allowed is not None:
            scores = jnp.where(allowed, scores, LOW)
        top_old = top[s, rows, :]
        top_new = jnp.maximum(top_old, jnp.max(scores, axis=-1, keepdims=True) * SCALE)
        shrink = jnp.exp2(top_old - top_new)
        span = scores.shape[1]
        anchor = top_new[:, 0:1] if span % WIDTH else jnp.tile(top_new, (1, span // WIDTH))
        weights = jnp.exp2(scores * SCALE - anchor).astype(BF16)
        top[s, rows, :] = top_new
        acc[s, rows, :] = acc[s, rows, :] * jnp.concatenate([shrink, shrink], axis=1) + jnp.dot(
            weights, vals, preferred_element_type=F32
        )

    def main_rows(s, items, halves):
        k0, v0 = values(0, *items)
        for j in range(HALF // BLOCK):
            update(s, HALF + j * BLOCK, BLOCK, k0, v0)
        for item, h in zip(items, halves):
            kh, vh = values(h, item)
            for j in range(HALF // BLOCK):
                update(s, pl.multiple_of(h * HALF + j * BLOCK, BLOCK), BLOCK, kh, vh)

    def sampled(item, carry):
        for half in range(2):
            first = item % 2 * 2
            kk, vv = values(half, (plane_at(first), item // 2), (plane_at(first + 1), item // 2))
            for s in range(4):
                update(s, MAIN, DEC, kk, vv)
        return carry

    def which(s, k, p):
        far = (x + NX - s) % NX
        return jnp.where(k == 0, jnp.where(x < far, 0, 1), jnp.where(p < z, 0, 1))

    def eye(n):
        return lax.broadcasted_iota(jnp.int32, (n, WIDTH), 0) == lax.broadcasted_iota(jnp.int32, (n, WIDTH), 1)

    def finish(s, r0, n, target, starget, row, count):
        rows = pl.ds(r0, n)
        total = acc[s, rows, WIDTH : 2 * WIDTH]
        target[rows, :] = (acc[s, rows, 0:WIDTH] / jnp.maximum(total, 1e-30)).astype(BF16)
        mask = eye(n)
        starget[row : row + 1, :] = jnp.sum(jnp.where(mask, top[s, rows, :], 0.0), axis=0, keepdims=True)
        starget[row + count : row + count + 1, :] = jnp.sum(jnp.where(mask, total, 0.0), axis=0, keepdims=True)

    def merge(s, r0, n, source, ssource, row, count):
        rows = pl.ds(r0, n)
        mask = eye(n)

        def column(r):
            return jnp.sum(jnp.where(mask, ssource[r : r + 1, :], 0.0), axis=1, keepdims=True)

        top_in, sum_in = column(row), column(row + count)
        top_old = top[s, rows, :]
        top_new = jnp.maximum(top_old, top_in)
        shrink = jnp.exp2(top_old - top_new)
        gain = jnp.exp2(top_in - top_new) * sum_in
        top[s, rows, :] = top_new
        acc[s, rows, 0:WIDTH] = acc[s, rows, 0:WIDTH] * shrink + source[rows, :].astype(F32) * gain
        acc[s, rows, WIDTH : 2 * WIDTH] = acc[s, rows, WIDTH : 2 * WIDTH] * shrink + gain

    def section(c):
        if c < 2:
            return [(c * HALF + j * BLOCK, BLOCK, c, j) for j in range(4)], 4, pl.ds(c * HALF, HALF), pl.ds(c, 1)
        half = DEC // 2
        return [(MAIN + j * half, half, 2 + j, 0) for j in range(2)], 1, pl.ds(MAIN, DEC), pl.ds(2, 2)

    def final_copies(s, c):
        _, _, rows, sheets = section(c)
        i, owner = 3 * (s - 1) + c, at(z, (x + NX - s) % NX, y)
        return [
            send(part.at[s, rows, :], got.at[s - 1, rows, :], fs.at[i], fr.at[i], owner),
            send(stat.at[s, sheets], gstat.at[s - 1, sheets], fs.at[9 + i], fr.at[9 + i], owner),
        ]

    def give(s, c):
        blocks, count, _, _ = section(c)
        for r0, n, sheet, j in blocks:
            finish(s, r0, n, part.at[s], stat.at[s, sheet], j, count)
        start(final_copies(s, c))

    def take(s, c):
        arrive(final_copies(s, c))
        blocks, count, _, _ = section(c)
        for r0, n, sheet, j in blocks:
            merge(0, r0, n, got.at[s - 1], gstat.at[s - 1, sheet], j, count)

    def give_sampled(s, carry):
        give(s, 2)
        return carry

    def take_sampled(s, carry):
        take(s, 2)
        return carry

    def d_copy(j):
        return send(dgat.at[0], dgat.at[j], ds.at[j - 1], dr.at[j - 1], along_y[j])

    def place(j):
        column = pl.multiple_of(((y + NY - j) % NY) * WIDTH, WIDTH)
        dout[:, pl.ds(column, WIDTH)] = dgat[j]

    z_step(0)
    q_copy(1).start()
    q_copy(3).start()

    y_step(0, 1)
    z_step(1)

    def clear(s, carry):
        acc[s] = jnp.zeros((ROWS, 2 * WIDTH), F32)
        top[s] = jnp.full((ROWS, WIDTH), LOW, F32)
        return carry

    lax.fori_loop(0, 4, clear, 0)

    step_row = lax.broadcasted_iota(jnp.int32, (DEC, DEC), 0)
    step_col = lax.broadcasted_iota(jnp.int32, (DEC, DEC), 1)
    own_v = dqkv[2]
    update(
        0, MAIN, DEC, dqkv[1], jnp.concatenate([own_v, jnp.ones_like(own_v)], axis=1),
        (step_row // 4 == step_col // 4) & (step_col <= step_row),
    )

    def own_plane(group):
        shape = (BLOCK, PART)
        key = group * PART + lax.broadcasted_iota(jnp.int32, shape, 1)
        key_slot = key // TOK
        key_delta = jnp.where(key_slot % 2 == 1, NY - (key_slot + 1) // 2, key_slot // 2)
        key_index = ((y + key_delta) % NY) * TOK + key % TOK
        query_index = y * TOK + lax.broadcasted_iota(jnp.int32, shape, 0) % TOK
        k0, v0 = values(0, (planes[0], group))
        k1, v1 = values(1, (planes[0], group))
        for j in range(HALF // BLOCK):
            update(0, HALF + j * BLOCK, BLOCK, k0, v0)
            update(0, j * BLOCK, BLOCK, k0, v0, key_index <= query_index)
        for j in range(HALF // BLOCK):
            update(0, HALF + j * BLOCK, BLOCK, k1, v1, key_index >= query_index)

    y_step(0, 2)
    q_copy(2).start()
    z_step(2)
    z_step(3)
    y_step(1, 1)

    unit_rows = (0, 1, 3, 0, 1, 3, 2, 2, 2, 2, 1, 1, 3, 3, 0, 0)
    unit_one = (0, 0, 0, 2, 4, 4, 0, 4, 1, 5, 1, 5, 1, 5, 6, 5)
    unit_two = (0, 2, 2, 4, 6, 6, 2, 6, 3, 7, 3, 7, 3, 7, 3, 7)

    def lookup(table, t):
        value = jnp.int32(table[0])
        for i in range(1, len(table)):
            value = jnp.where(t == i, table[i], value)
        return value

    def sampled_out():
        lax.fori_loop(1, NX, take_sampled, 0)
        rows = pl.ds(MAIN, DEC)
        dgat[0] = (acc[0, rows, 0:WIDTH] / acc[0, rows, WIDTH : 2 * WIDTH]).astype(BF16)
        start([d_copy(j) for j in range(1, NY)])
        place(0)

    after = {
        0: [lambda: y_step(0, 3), lambda: y_step(2, 1), lambda: y_step(3, 1), lambda: y_step(1, 2)],
        1: [lambda: y_step(0, 4), lambda: y_step(2, 2)],
        2: [lambda: y_step(3, 2)],
        3: [lambda: y_step(1, 3)],
        4: [lambda: y_step(2, 3)],
        5: [lambda: y_step(3, 3)],
        7: [lambda: far_step(1)],
        8: [lambda: far_step(2), lambda: far_step(3)],
        11: [sampled_out],
    }
    met = (0, 0, 0, 0, 0, 0, 1, 3, 4, 4, 4, 4, 4, 4, 4, 4)

    before = {
        1: [lambda: q_copy(1).wait_recv()],
        2: [lambda: q_copy(3).wait_recv()],
        6: [lambda: q_copy(2).wait_recv()],
    }

    def hook(table, t):
        for i, work in table.items():

            @pl.when(t == i)
            def _(work=work):
                for step in work:
                    step()

    def unit(t, carry):
        hook(before, t)
        s = lookup(unit_rows, t)

        @pl.when((t == 0) | (t == 14))
        def _():
            own_plane(jnp.where(t == 0, 0, 1))

        @pl.when(t > 0)
        def _():
            items, halves = [], []
            for table in (unit_one, unit_two):
                item = lookup(table, t)
                k, group = item // 2, item % 2
                p = plane_at(k)
                items.append((p, group))
                halves.append(which(s, k, p))
            main_rows(s, items, halves)

        hook(after, t)
        lax.fori_loop(lookup(met, t - 1), lookup(met, t), sampled, 0)

        @pl.when(t == 8)
        def _():
            lax.fori_loop(1, NX, give_sampled, 0)

        @pl.when((t == 9) | (t == 11) | (t == 13))
        def _():
            give(s, 0)
            give(s, 1)

        return carry

    lax.fori_loop(0, 16, unit, 0)

    def take_main(i, carry):
        s = lookup((2, 1, 3), i)
        take(s, 0)
        take(s, 1)
        return carry

    lax.fori_loop(0, 3, take_main, 0)
    for c in range(2):
        for g in range(GROUP):
            rows = pl.ds(c * HALF + g * TOK, TOK)
            out[c, :, g * WIDTH : (g + 1) * WIDTH] = (
                acc[0, rows, 0:WIDTH] / acc[0, rows, WIDTH : 2 * WIDTH]
            ).astype(BF16)
    for j in range(1, NY):
        d_copy(j).wait_recv()
        place(j)

    gone = [z_copy(i, r) for i in range(1, NZ) for r in (0, 7)]
    gone += [q_copy(j) for j in range(1, NX)] + [d_copy(j) for j in range(1, NY)]
    for k in range(NZ):
        for copies in steps(k):
            gone += copies
    for s in range(1, NX):
        for c in range(3):
            gone += final_copies(s, c)
    for copy in gone:
        copy.wait_send()


def local(prompt_q, prompt_k, prompt_v, dec_q, dec_k, dec_v):
    head = lax.axis_index("seq") * WIDTH
    mine = lax.dynamic_slice_in_dim(dec_q, head, WIDTH, 2)
    dqkv = jnp.stack([mine, dec_k, dec_v]).reshape(3, DEC, WIDTH)
    vmem = pl.BlockSpec(memory_space=pltpu.VMEM)
    dma = pltpu.SemaphoreType.DMA
    prefill_out, decode_out = pl.pallas_call(
        kernel,
        out_shape=(
            jax.ShapeDtypeStruct((2, TOK, GROUP * WIDTH), BF16),
            jax.ShapeDtypeStruct((DEC, GROUP * WIDTH), BF16),
        ),
        in_specs=[vmem] * 4,
        out_specs=(vmem, vmem),
        scratch_shapes=[
            pltpu.VMEM((4, ROWS, WIDTH), BF16),
            pltpu.VMEM((NZ, 2, 2, PART, 2 * WIDTH), BF16),
            pltpu.VMEM((4, ROWS, 2 * WIDTH), F32),
            pltpu.VMEM((4, ROWS, WIDTH), F32),
            pltpu.VMEM((4, ROWS, WIDTH), BF16),
            pltpu.VMEM((4, 4, 8, WIDTH), F32),
            pltpu.VMEM((3, ROWS, WIDTH), BF16),
            pltpu.VMEM((3, 4, 8, WIDTH), F32),
            pltpu.VMEM((NY, DEC, WIDTH), BF16),
            dma((2 * NZ - 2,)),
            dma((NZ, 2)),
            dma((NZ, 8)),
            dma((NZ, 8)),
            dma((NX - 1,)),
            dma((NX - 1,)),
            dma((18,)),
            dma((18,)),
            dma((NY - 1,)),
            dma((NY - 1,)),
        ],
        compiler_params=pltpu.CompilerParams(
            collective_id=0, has_side_effects=True, vmem_limit_bytes=48 << 20
        ),
    )(prompt_q, prompt_k, prompt_v, dqkv)
    return prefill_out, decode_out.reshape(dec_q.shape)


def solution(mesh):
    placed = (
        P(None, ("rep", "seq"), "tp"),
        P(None, ("rep", "seq"), "tp"),
        P(None, ("rep", "seq"), "tp"),
        P("rep", None, "tp"),
        P("rep", None, "tp"),
        P("rep", None, "tp"),
    )
    return jax.shard_map(
        local,
        mesh=mesh,
        in_specs=placed,
        out_specs=(P(None, ("rep", "seq"), "tp"), P("rep", None, "tp")),
        check_vma=False,
    )
```
